32 devices in a mesh: dp: 8 (over z, y), seq: 4 (over x, core).
Axes of the slice: x: 2, y: 2, z: 4, core: 2. Of those that a mesh axis runs over, the one named last changes fastest.
Arguments:
- acts: bfloat16 [16, 512, 4608], P('dp', 'seq'), may hold values from -20 to 20, as said below
- grads: bfloat16 [16, 512, 18432], P('dp', 'seq'), may hold values from -0.00045670236 to 0.00045670236, as said below
Outputs:
- update: bfloat16 [4608, 18432], P('dp', 'seq')
- norms: float32 [16], P('dp')
The draws below stay inside these ranges and needn't reach their ends.
Inputs may be any that keep to these rules, and one draw needn't show every extreme that they name: `acts`: entries of order one. `grads`: independent entries, small: magnitudes under 2000 / (21 * sqrt(43486543872)).
All inputs are finite; a program needn't handle non-finite values.
Results may differ from the reference program's by a relative error of at most 0.025.
Values may be sent and summed in bfloat16 or wider, within the bound.
A program may use at most 192 MiB of HBM per device.

```python
import math
import jax
import jax.numpy as jnp
from jax import lax

D = 4608
FF = 18432
LEN = 512
SEQ_DEV = 2
SEQS = 16
N_DP = 8


def draw_acts(key, part):
    key = jax.random.fold_in(key, 11)
    knoise, krow, kcol = jax.random.split(key, 3)
    row_clip_scale = jnp.exp(jax.random.uniform(krow, (SEQS, LEN, 1), jnp.float32) * math.log(10.0))
    col_scale = jnp.exp(jax.random.uniform(kcol, (1, 1, D), jnp.float32) * math.log(10.0))
    base = jnp.clip(jax.random.normal(knoise, (SEQS, LEN, D), jnp.float32), -4.0, 4.0)
    return (base * row_clip_scale * col_scale / 21.0).astype(jnp.bfloat16)


def rising(count, slope):
    position = jnp.arange(count, dtype=jnp.float32) / (count - 1)
    return (1.0 + slope * position) / (1.0 + slope)


def draw_grads(key, part):
    key = jax.random.fold_in(key, 23)
    knoise, krow, kcol, kexample = jax.random.split(key, 4)
    row_clip_scale = jnp.exp(jax.random.uniform(krow, (SEQS, LEN, 1), jnp.float32) * math.log(10.0))
    col_scale = jnp.exp(jax.random.uniform(kcol, (1, 1, FF), jnp.float32) * math.log(10.0))
    example_scale = jnp.exp(jax.random.uniform(kexample, (SEQS, 1, 1), jnp.float32, math.log(0.3), math.log(3.0)))
    token_ramp = rising(LEN, 2.0).reshape(1, LEN, 1)
    column_ramp = rising(FF, 2.0).reshape(1, 1, FF)
    base = jnp.clip(jax.random.normal(knoise, (SEQS, LEN, FF), jnp.float32), -4.0, 4.0)
    scale = example_scale * token_ramp * column_ramp * 1.44 / (21.0 * math.sqrt(LEN * D * FF))
    return (base * row_clip_scale * col_scale * scale).astype(jnp.bfloat16)


def setup_inputs(seed: int = 0) -> dict:
    keys = jax.random.split(jax.random.key(seed), 3)
    acts = draw_acts(jax.random.fold_in(keys[2], 71), 0)
    grads = draw_grads(jax.random.fold_in(keys[2], 71), 0)
    return dict(acts=acts, grads=grads)


def per_example_norm(pair):
    x, g = pair
    xf = x.astype(jnp.float32)
    gf = g.astype(jnp.float32)
    activation_gram_matrix = jnp.dot(xf, xf.T, preferred_element_type=jnp.float32)
    gradient_gram_matrix = jnp.dot(gf, gf.T, preferred_element_type=jnp.float32)
    return jnp.sqrt(jnp.sum(activation_gram_matrix * gradient_gram_matrix))

def reference(acts, grads):
    norms = lax.map(per_example_norm, (acts, grads))
    clip = jnp.minimum(1.0, 1.0 / (norms + 1e-06))
    factor = math.sqrt(D * FF / SEQS)
    scaled = (grads * (clip * factor)[:, None, None]).astype(jnp.bfloat16)
    group_x = acts.reshape(N_DP, SEQ_DEV * LEN, D)
    group_z = scaled.reshape(N_DP, SEQ_DEV * LEN, FF)

    def add_group(total, pair):
        x, z = pair
        term = jnp.dot(x.astype(jnp.float32).T, z.astype(jnp.float32), preferred_element_type=jnp.float32)
        return (total + term.astype(jnp.bfloat16).astype(jnp.float32), None)
    total, _ = lax.scan(add_group, jnp.zeros((D, FF), jnp.float32), (group_x, group_z))
    return (total.astype(jnp.bfloat16), norms)
```

```python
import functools
import math

import jax
import jax.numpy as jnp
from jax import lax
from jax.experimental import pallas as pl
from jax.experimental.pallas import tpu as pltpu
from jax.sharding import PartitionSpec as P

MESH = pl.DeviceIdType.MESH
PARTS = 3


def flip(value, bit):
    return value + bit * (1 - 2 * ((value // bit) % 2))


def xor(value, mask):
    bit = 1
    while bit <= mask:
        if mask & bit:
            value = flip(value, bit)
        bit *= 2
    return value


def powers(count, first):
    found, bit = [], 1
    while bit < count:
        found.append(bit * first)
        bit *= 2
    return found


def split_of(dp, seq, hidden):
    lanes = dp // 2
    while (hidden // seq) % (lanes * 128):
        lanes //= 2
    return lanes


def gather_kernel(L, seq, acts, grads, a_all, b_all,
                  a_send, a_recv, f_send, f_recv, b_send, b_recv, own_sem):
    d, s = lax.axis_index("dp"), lax.axis_index("seq")
    h, l = d // L, d % L
    E, T, D = acts.shape
    nb = b_all.shape[2]
    W = D // PARTS
    bits = [("s", m) for m in powers(seq // 2, 2)] + [("l", m) for m in powers(L, 1)]
    n = len(bits)
    blocks = 1 << n

    def relative(mask, order, core=0):
        ll, ss = l, s
        for j in range(n):
            if mask >> j & 1:
                kind, m = order[j]
                if kind == "s":
                    ss = flip(ss, m)
                else:
                    ll = flip(ll, m)
        if core:
            ss = flip(ss, 1)
        return ll, ss

    barrier = pltpu.get_barrier_semaphore()
    for mask in range(blocks):
        for core in range(2):
            if mask or core:
                ll, ss = relative(mask, bits, core)
                pl.semaphore_signal(barrier, inc=1, device_id=(h * L + ll, ss), device_id_type=MESH)
    pl.semaphore_wait(barrier, 2 * blocks - 1)

    def a_at(ll, ss, r):
        return a_all.at[pl.ds(ll * E, E), pl.ds(ss * T, T), pl.ds(r * W, W)]

    def order_of(r):
        return bits[r % n:] + bits[:r % n]

    def a_copy(r, mask, k):
        order = order_of(r)
        src = acts.at[:, :, pl.ds(r * W, W)] if mask == 0 else a_at(*relative(mask, order), r)
        tl, ts = relative(1 << k, order)
        land = mask | 1 << k
        return pltpu.make_async_remote_copy(
            src_ref=src, dst_ref=a_at(*relative(mask, order), r),
            send_sem=a_send.at[r, land], recv_sem=a_recv.at[r, land],
            device_id=(h * L + tl, ts), device_id_type=MESH)

    def f_copy(r, mask):
        order = order_of(r)
        src = acts.at[:, :, pl.ds(r * W, W)] if mask == 0 else a_at(*relative(mask, order), r)
        tl, ts = relative(0, order, 1)
        return pltpu.make_async_remote_copy(
            src_ref=src, dst_ref=a_at(*relative(mask, order), r),
            send_sem=f_send.at[r, mask], recv_sem=f_recv.at[r, mask],
            device_id=(h * L + tl, ts), device_id_type=MESH)

    def landed(ref, sems, *index):
        return pltpu.make_async_remote_copy(
            src_ref=ref, dst_ref=ref, send_sem=sems.at[index], recv_sem=sems.at[index],
            device_id=(d, s), device_id_type=MESH)

    def b_copy(mask, core):
        tl, ts = relative(mask, bits, core)
        column = pl.multiple_of((ts * L + tl) * nb, 128)
        return pltpu.make_async_remote_copy(
            src_ref=grads.at[:, :, pl.ds(column, nb)],
            dst_ref=b_all.at[pl.ds(l * E, E), pl.ds(s * T, T), :],
            send_sem=b_send.at[mask, core], recv_sem=b_recv.at[mask, core],
            device_id=(h * L + tl, ts), device_id_type=MESH)

    started = []

    def go(copy):
        copy.start()
        started.append(copy)

    for k in range(n):
        for r in range(PARTS):
            go(a_copy(r, 0, k))
    own_a = pltpu.make_async_copy(
        acts, a_all.at[pl.ds(l * E, E), pl.ds(s * T, T), :], own_sem.at[0])
    own_a.start()
    column = pl.multiple_of((s * L + l) * nb, 128)
    own_b = pltpu.make_async_copy(
        grads.at[:, :, pl.ds(column, nb)],
        b_all.at[pl.ds(l * E, E), pl.ds(s * T, T), :], own_sem.at[1])
    own_b.start()
    for r in range(PARTS):
        go(f_copy(r, 0))
    to_send = sorted(
        ((m, c) for m in range(blocks) for c in range(2) if m or c),
        key=lambda mc: -bin(mc[0]).count("1"))
    half = len(to_send) // 2
    for mc in to_send[:half]:
        go(b_copy(*mc))
    arrivals = sorted(range(1, blocks), key=lambda m: (bin(m).count("1"), m))
    seen = 0
    for mask in arrivals:
        for r in range(PARTS):
            order = order_of(r)
            landed(a_at(*relative(mask, order), r), a_recv, r, mask).wait_recv()
            for k in range(mask.bit_length(), n):
                go(a_copy(r, mask, k))
            go(f_copy(r, mask))
        seen += 1
        if seen == n:
            for mc in to_send[half:]:
                go(b_copy(*mc))
    if seen < n:
        for mc in to_send[half:]:
            go(b_copy(*mc))
    for r in range(PARTS):
        order = order_of(r)
        for mask in range(blocks):
            landed(a_at(*relative(mask, order, 1), r), f_recv, r, mask).wait_recv()
    for mask, core in to_send:
        ll, ss = relative(mask, bits, core)
        landed(b_all.at[pl.ds(ll * E, E), pl.ds(ss * T, T), :], b_recv, mask, core).wait_recv()
    for copy in started:
        copy.wait_send()
    own_a.wait()
    own_b.wait()


def gather(L, seq, acts, grads):
    E, T, D = acts.shape
    nb = grads.shape[2] // (seq * L)
    blocks = L * seq // 2
    dma = pltpu.SemaphoreType.DMA
    return pl.pallas_call(
        functools.partial(gather_kernel, L, seq),
        out_shape=(
            jax.ShapeDtypeStruct((L * E, seq * T, D), acts.dtype),
            jax.ShapeDtypeStruct((L * E, seq * T, nb), grads.dtype),
        ),
        in_specs=[pl.BlockSpec(memory_space=pl.ANY)] * 2,
        out_specs=(pl.BlockSpec(memory_space=pl.ANY),) * 2,
        scratch_shapes=[
            dma((PARTS, blocks)), dma((PARTS, blocks)),
            dma((PARTS, blocks)), dma((PARTS, blocks)),
            dma((blocks, 2)), dma((blocks, 2)), dma((2,)),
        ],
        compiler_params=pltpu.CompilerParams(collective_id=0, has_side_effects=True),
        name="gather_tokens",
    )(acts, grads)


def product_kernel(H, L, RB, TM, a_ref, b_ref, out, a_buf, b_buf, c_buf, recv,
                   a_sem, b_sem, s_send, s_recv, o_send, o_recv, own_sem):
    d, s = lax.axis_index("dp"), lax.axis_index("seq")
    h, l = d // L, d % L
    K, D = a_ref.shape
    nb = b_ref.shape[1]
    tiles, k = D // TM, TM // RB
    b_load = pltpu.make_async_copy(b_ref, b_buf, b_sem)
    b_load.start()
    whole_tiles = L % k == 0
    plan = []
    if whole_tiles:
        per = L // k
        for o in list(range(1, H)) + [0]:
            hh = (h + o) % H
            for i in reversed(range(per)):
                tile = hh * per + xor(l // k, i)
                plan.append((tile, [(tile * k + xor(l % k, j), o != 0) for j in reversed(range(k))]))
    else:
        first = (h + 1) * L // k
        for i in range(tiles):
            tile = (first + i) % tiles
            plan.append((tile, [(tile * k + j, None) for j in range(k)]))

    def a_load(i):
        column = pl.multiple_of(plan[i][0] * TM, 128)
        return pltpu.make_async_copy(a_ref.at[:, pl.ds(column, TM)], a_buf.at[i % 2], a_sem.at[i % 2])

    a_load(0).start()
    barrier = pltpu.get_barrier_semaphore()
    for o in range(1, H):
        pl.semaphore_signal(barrier, inc=1, device_id=((h + o) % H * L + l, s), device_id_type=MESH)
    for i in range(1, L):
        pl.semaphore_signal(barrier, inc=1, device_id=(h * L + xor(l, i), s), device_id_type=MESH)
    pl.semaphore_wait(barrier, H + L - 2)

    def s_copy(block):
        hh, ll = block // L, block % L
        slot = (h - hh + H) % H - 1
        return pltpu.make_async_remote_copy(
            src_ref=c_buf.at[pl.ds(pl.multiple_of(block * RB, 16), RB)],
            dst_ref=recv.at[slot, pl.ds(pl.multiple_of(ll * RB, 16), RB)],
            send_sem=s_send.at[block], recv_sem=s_recv.at[slot, ll],
            device_id=(hh * L + l, s), device_id_type=MESH)

    chunk = 384
    for i, (tile, rows) in enumerate(plan):
        if i + 1 < tiles:
            a_load(i + 1).start()
        a_load(i).wait()
        if i == 0:
            b_load.wait()

        @pl.loop(0, TM // chunk)
        def _(m):
            column = pl.multiple_of(m * chunk, 128)
            value = lax.dot_general(
                a_buf[i % 2, :, pl.ds(column, chunk)], b_buf[...],
                (((0,), (0,)), ((), ())), preferred_element_type=jnp.float32)
            row = pl.multiple_of(tile * TM + m * chunk, 128)
            c_buf[pl.ds(row, chunk), :] = value.astype(jnp.bfloat16)

        for block, away in rows:
            if away is None:
                @pl.when(block // L != h)
                def _():
                    s_copy(block).start()
            elif away:
                s_copy(block).start()

    def o_copy(i):
        ll = xor(l, i)
        src = c_buf.at[pl.ds(pl.multiple_of((h * L + ll) * RB, 16), RB)]
        return pltpu.make_async_remote_copy(
            src_ref=src, dst_ref=out.at[:, pl.ds(pl.multiple_of(l * nb, 128), nb)],
            send_sem=o_send.at[i], recv_sem=o_recv.at[i],
            device_id=(h * L + ll, s), device_id_type=MESH)

    own = pltpu.make_async_copy(
        c_buf.at[pl.ds(pl.multiple_of((h * L + l) * RB, 16), RB)],
        out.at[:, pl.ds(pl.multiple_of(l * nb, 128), nb)], own_sem)
    step = 96
    for i in reversed(range(L)):
        ll = xor(l, i)
        for slot in range(H - 1):
            land = recv.at[slot, pl.ds(pl.multiple_of(ll * RB, 16), RB)]
            pltpu.make_async_remote_copy(
                src_ref=land, dst_ref=land, send_sem=s_recv.at[slot, ll],
                recv_sem=s_recv.at[slot, ll], device_id=(d, s), device_id_type=MESH).wait_recv()

        @pl.loop(0, RB // step)
        def _(m):
            here = pl.ds(pl.multiple_of((h * L + ll) * RB + m * step, 16), step)
            there = pl.ds(pl.multiple_of(ll * RB + m * step, 16), step)
            total = c_buf[here, :].astype(jnp.float32)
            for slot in range(H - 1):
                total = total + recv[slot, there, :].astype(jnp.float32)
            c_buf[here, :] = total.astype(jnp.bfloat16)

        if i:
            o_copy(i).start()
        else:
            own.start()
    for o in range(1, H):
        for ll in range(L):
            s_copy((h + o) % H * L + ll).wait_send()
    for i in range(1, L):
        land = out.at[:, pl.ds(pl.multiple_of(xor(l, i) * nb, 128), nb)]
        pltpu.make_async_remote_copy(
            src_ref=land, dst_ref=land, send_sem=o_recv.at[i], recv_sem=o_recv.at[i],
            device_id=(d, s), device_id_type=MESH).wait_recv()
        o_copy(i).wait_send()
    own.wait()


def product(dp, seq, L, a_all, b_all):
    K, D = a_all.shape
    nb = b_all.shape[1]
    H, RB = dp // L, D // dp
    TM = math.lcm(RB, 128)
    dma = pltpu.SemaphoreType.DMA
    return pl.pallas_call(
        functools.partial(product_kernel, H, L, RB, TM),
        out_shape=jax.ShapeDtypeStruct((RB, nb * L), jnp.bfloat16),
        in_specs=[pl.BlockSpec(memory_space=pl.ANY)] * 2,
        out_specs=pl.BlockSpec(memory_space=pl.ANY),
        scratch_shapes=[
            pltpu.VMEM((2, K, TM), jnp.bfloat16),
            pltpu.VMEM((K, nb), jnp.bfloat16),
            pltpu.VMEM((D, nb), jnp.bfloat16),
            pltpu.VMEM((H - 1, L * RB, nb), jnp.bfloat16),
            dma((2,)), dma, dma((dp,)), dma((H - 1, L)), dma((L,)), dma((L,)), dma,
        ],
        compiler_params=pltpu.CompilerParams(
            collective_id=1, has_side_effects=True, vmem_limit_bytes=60 * 2**20),
        cost_estimate=pl.CostEstimate(
            flops=2 * K * D * nb, bytes_accessed=2 * (K * D + K * nb + RB * nb * L), transcendentals=0),
        name="product_scatter",
    )(a_all, b_all)


def on_device(acts, grads):
    seq, dp = lax.axis_size("seq"), lax.axis_size("dp")
    examples, local_len, width = acts.shape
    hidden = grads.shape[2]
    L = split_of(dp, seq, hidden)
    d = lax.axis_index("dp")
    a_all, b_all = gather(L, seq, acts, grads)
    act_gram = jnp.einsum("nih,nfh->nif", a_all, a_all, preferred_element_type=jnp.float32)
    grad_gram = jnp.einsum("nih,nfh->nif", b_all, b_all, preferred_element_type=jnp.float32)
    part = jnp.sum(act_gram * grad_gram, axis=(1, 2))
    here = d // L * (L * examples)
    every = lax.dynamic_update_slice(jnp.zeros((dp * examples,), jnp.float32), part, (here,))
    norms = jnp.sqrt(lax.psum(every, ("dp", "seq")))
    clip = jnp.minimum(1.0, 1.0 / (norms + 1e-06))
    factor = math.sqrt(width * hidden / (examples * dp))
    scale = lax.dynamic_slice(clip * factor, (here,), (L * examples,))
    scaled = (b_all * scale[:, None, None]).astype(jnp.bfloat16)
    tokens = L * examples * seq * local_len
    update = product(dp, seq, L, a_all.reshape(tokens, width), scaled.reshape(tokens, -1))
    return update, lax.dynamic_slice(norms, (d * examples,), (examples,))


def solution(mesh):
    return jax.shard_map(
        on_device,
        mesh=mesh,
        in_specs=(P("dp", "seq", None), P("dp", "seq", None)),
        out_specs=(P("dp", "seq"), P("dp")),
        check_vma=False,
    )
```

```python
import functools
import math

import jax
import jax.numpy as jnp
from jax import lax
from jax.experimental import pallas as pl
from jax.experimental.pallas import tpu as pltpu
from jax.sharding import PartitionSpec as P

MESH = pl.DeviceIdType.MESH


def flip(value, bit):
    return value + bit * (1 - 2 * ((value // bit) % 2))


def xor(value, mask):
    bit = 1
    while bit <= mask:
        if mask & bit:
            value = flip(value, bit)
        bit *= 2
    return value


def split_of(dp, seq, hidden):
    lanes = dp // 2
    while (hidden // seq) % (lanes * 128):
        lanes //= 2
    return lanes


def steps_of(H, L, RB, TM, D, h):
    tiles, k = D // TM, TM // RB
    first = (h + 1) * L // k
    return [(first + i) % tiles for i in range(tiles)]


def leader(l, c, n, mask):
    mirrored = sum(1 << (n - 1 - j) for j in range(n) if mask >> j & 1)
    return (1 - c) * xor(l, mask) + c * xor(l, mirrored)


def landed(ref, sem, d, s):
    return pltpu.make_async_remote_copy(
        src_ref=ref, dst_ref=ref, send_sem=sem, recv_sem=sem, device_id=(d, s), device_id_type=MESH)


class Spread:
    def __init__(self, h, l, s, L, own, buf, sems, copies):
        self.h, self.l, self.s, self.c, self.L = h, l, s, s % 2, L
        self.n = L.bit_length() - 1
        self.own, self.buf, self.copies = own, buf, copies
        self.t_send, self.t_recv, self.f_send, self.f_recv, self.local_sem = sems

    def at(self, ll, core):
        return self.buf.at[2 * ll + core]

    def send(self, mask, k):
        ll = leader(self.l, self.c, self.n, mask)
        land = mask | 1 << k
        copy = pltpu.make_async_remote_copy(
            src_ref=self.at(ll, self.c) if mask else self.own(self.c), dst_ref=self.at(ll, self.c),
            send_sem=self.t_send.at[land], recv_sem=self.t_recv.at[land],
            device_id=(self.h * self.L + leader(self.l, self.c, self.n, 1 << k), self.s),
            device_id_type=MESH)
        copy.start()
        self.copies.append(copy)

    def begin(self):
        for k in range(self.n):
            self.send(0, k)
        self.local = []
        for e in range(2):
            copy = pltpu.make_async_copy(self.own(e), self.at(self.l, e), self.local_sem.at[e])
            copy.start()
            self.local.append(copy)

    def forward(self):
        d = self.h * self.L + self.l
        for mask in sorted(range(1, 1 << self.n), key=lambda m: (bin(m).count("1"), m)):
            ll = leader(self.l, self.c, self.n, mask)
            here = self.at(ll, self.c)
            landed(here, self.t_recv.at[mask], d, self.s).wait_recv()
            for k in range(mask.bit_length(), self.n):
                self.send(mask, k)
            copy = pltpu.make_async_remote_copy(
                src_ref=here, dst_ref=here, send_sem=self.f_send.at[mask], recv_sem=self.f_recv.at[mask],
                device_id=(d, flip(self.s, 1)), device_id_type=MESH)
            copy.start()
            self.copies.append(copy)

    def finish(self):
        d = self.h * self.L + self.l
        for mask in range(1, 1 << self.n):
            ll = leader(self.l, 1 - self.c, self.n, mask)
            landed(self.at(ll, 1 - self.c), self.f_recv.at[mask], d, self.s).wait_recv()
        for copy in self.local:
            copy.wait()


def gather_kernel(H, L, seq, RB, TM, acts, grads, a_own, a_first, b_own, b_all,
                  a_send, a_recv, f_send, f_recv, b1_send, b1_recv, b2_send, b2_recv,
                  t_send, t_recv, tf_send, tf_recv, local_sem, own_sem):
    d, s = lax.axis_index("dp"), lax.axis_index("seq")
    h, l = d // L, d % L
    E, T, D = acts.shape
    nb = b_all.shape[2]
    tiles = steps_of(H, L, RB, TM, D, h)
    barrier = pltpu.get_barrier_semaphore()
    for q in range(1, seq):
        pl.semaphore_signal(barrier, inc=1, device_id=(d, xor(s, q)), device_id_type=MESH)
    for j in range(1, L):
        pl.semaphore_signal(barrier, inc=1, device_id=(h * L + xor(l, j), s), device_id_type=MESH)
    pl.semaphore_wait(barrier, seq + L - 2)

    copies = []

    def go(src, dst, send_sem, recv_sem, device):
        copy = pltpu.make_async_remote_copy(
            src_ref=src, dst_ref=dst, send_sem=send_sem, recv_sem=recv_sem,
            device_id=device, device_id_type=MESH)
        copy.start()
        copies.append(copy)

    def a_cols(i):
        return pl.ds(pl.multiple_of(tiles[i] * TM, 128), TM)

    def a_at(ss, i):
        return a_own.at[:, pl.ds(ss * T, T), a_cols(i)]

    def a_begin(i):
        src = acts.at[:, :, a_cols(i)]
        for q in range(2, seq, 2):
            go(src, a_at(s, i), a_send.at[i, q // 2], a_recv.at[i, q // 2], (d, xor(s, q)))
        go(src, a_at(s, i), f_send.at[i, 0], f_recv.at[i, 0], (d, flip(s, 1)))

    def a_forward(i):
        for q in range(2, seq, 2):
            here = a_at(xor(s, q), i)
            landed(here, a_recv.at[i, q // 2], d, s).wait_recv()
            go(here, here, f_send.at[i, q // 2], f_recv.at[i, q // 2], (d, flip(s, 1)))

    def a_finish(i):
        for q in range(0, seq, 2):
            landed(a_at(flip(xor(s, q), 1), i), f_recv.at[i, q // 2], d, s).wait_recv()

    def g_cols(ss, ll):
        return pl.ds(pl.multiple_of((ss * L + ll) * nb, 128), nb)

    def b_at(ss, j):
        return b_own.at[:, pl.ds(ss * T, T), pl.ds(pl.multiple_of(xor(l, j) * nb, 128), nb)]

    def b_out(ll, ss):
        return b_all.at[pl.ds(ll * E, E), pl.ds(ss * T, T), :]

    def b_begin(j):
        for q in reversed(range(1, seq)):
            ss = xor(s, q)
            go(grads.at[:, :, g_cols(ss, xor(l, j))], b_at(s, j),
               b1_send.at[q, j], b1_recv.at[q, j], (d, ss))

    def b_forward(q, j):
        ss = xor(s, q)
        if q:
            landed(b_at(ss, j), b1_recv.at[q, j], d, s).wait_recv()
        if j:
            src = b_at(ss, j) if q else grads.at[:, :, g_cols(s, xor(l, j))]
            go(src, b_out(l, ss), b2_send.at[q, j], b2_recv.at[q, j], (h * L + xor(l, j), s))

    a_begin(0)
    owns = [
        pltpu.make_async_copy(acts, a_own.at[:, pl.ds(s * T, T), :], own_sem.at[0]),
        pltpu.make_async_copy(
            grads.at[:, :, pl.ds(pl.multiple_of(s * L * nb, 128), L * nb)],
            b_own.at[:, pl.ds(s * T, T), :], own_sem.at[1]),
    ]
    for copy in owns:
        copy.start()
    for j in reversed(range(1, L)):
        b_begin(j)
        b_forward(0, j)
    b_begin(0)
    for i in range(1, len(tiles)):
        a_begin(i)
    a_forward(0)
    a_finish(0)
    for copy in owns:
        copy.wait()
    spread = Spread(h, l, s, L, lambda e: a_own.at[e, :, a_cols(0)], a_first,
                    (t_send, t_recv, tf_send, tf_recv, local_sem), copies)
    spread.begin()
    for j in reversed(range(1, L)):
        for q in range(1, seq):
            b_forward(q, j)
    spread.forward()
    for q in range(1, seq):
        b_forward(q, 0)
    mine = pltpu.make_async_copy(
        b_own.at[:, :, pl.ds(pl.multiple_of(l * nb, 128), nb)], b_all.at[pl.ds(l * E, E)], own_sem.at[2])
    mine.start()
    for i in range(1, len(tiles)):
        a_forward(i)
    for i in range(1, len(tiles)):
        a_finish(i)
    spread.finish()
    for j in range(1, L):
        for q in range(seq):
            landed(b_out(xor(l, j), xor(s, q)), b2_recv.at[q, j], d, s).wait_recv()
    mine.wait()
    for copy in copies:
        copy.wait_send()


def gather(dp, seq, L, acts, grads):
    E, T, D = acts.shape
    nb = grads.shape[2] // (seq * L)
    H, RB = dp // L, D // dp
    TM = math.lcm(RB, 128)
    tiles = D // TM
    dma = pltpu.SemaphoreType.DMA
    shape = lambda *sizes: jax.ShapeDtypeStruct(sizes, jnp.bfloat16)
    return pl.pallas_call(
        functools.partial(gather_kernel, H, L, seq, RB, TM),
        out_shape=(shape(E, seq * T, D), shape(L * E, seq * T, TM),
                   shape(E, seq * T, L * nb), shape(L * E, seq * T, nb)),
        in_specs=[pl.BlockSpec(memory_space=pl.ANY)] * 2,
        out_specs=(pl.BlockSpec(memory_space=pl.ANY),) * 4,
        scratch_shapes=[dma((tiles, seq // 2))] * 4 + [dma((seq, L))] * 4 + [dma((L,))] * 4
        + [dma((2,)), dma((3,))],
        compiler_params=pltpu.CompilerParams(collective_id=0, has_side_effects=True),
        name="gather_tokens",
    )(acts, grads)


def product_kernel(H, L, seq, RB, TM, factor, part, a_own, a_first, b_ref, out, norms, a_rest,
                   a_buf, b_buf, c_buf, recv, slots, n_send, n_recv, t_send, t_recv, tf_send, tf_recv,
                   local_sem, a_sem, b_sem, s_send, s_recv, o_send, o_recv, own_sem):
    d, s = lax.axis_index("dp"), lax.axis_index("seq")
    h, l = d // L, d % L
    D = a_own.shape[2]
    examples, tokens, nb = b_ref.shape
    tiles, k = D // TM, TM // RB
    order = steps_of(H, L, RB, TM, D, h)
    b_load = pltpu.make_async_copy(b_ref, b_buf, b_sem)
    b_load.start()

    def a_load(i):
        src = a_first if i == 0 else a_rest.at[i - 1]
        return pltpu.make_async_copy(src, a_buf.at[i % 2], a_sem.at[i % 2])

    a_load(0).start()
    group = [(j, q) for j in range(L) for q in range(seq) if j or q]
    barrier = pltpu.get_barrier_semaphore()
    for o in range(1, H):
        pl.semaphore_signal(barrier, inc=1, device_id=((h + o) % H * L + l, s), device_id_type=MESH)
    for j, q in group:
        pl.semaphore_signal(barrier, inc=1, device_id=(h * L + xor(l, j), xor(s, q)), device_id_type=MESH)
    pl.semaphore_wait(barrier, H - 1 + len(group))

    copies = []
    for j, q in group:
        copy = pltpu.make_async_remote_copy(
            src_ref=part, dst_ref=slots.at[l * seq + s],
            send_sem=n_send.at[j, q], recv_sem=n_recv.at[j, q],
            device_id=(h * L + xor(l, j), xor(s, q)), device_id_type=MESH)
        copy.start()
        copies.append(copy)
    slots[l * seq + s] = part[...]

    def spread_of(i):
        column = pl.ds(pl.multiple_of(order[i] * TM, 128), TM)
        return Spread(h, l, s, L, lambda e: a_own.at[e, :, column], a_rest.at[i - 1],
                      tuple(x.at[i - 1] for x in (t_send, t_recv, tf_send, tf_recv, local_sem)), copies)

    spreads = [None] + [spread_of(i) for i in range(1, tiles)]
    for spread in spreads[1:]:
        spread.begin()

    for j, q in group:
        landed(slots.at[xor(l, j) * seq + xor(s, q)], n_recv.at[j, q], d, s).wait_recv()
    b_load.wait()
    part_rows = 64
    for ll in range(L):
        total = slots[ll * seq]
        for ss in range(1, seq):
            total = total + slots[ll * seq + ss]
        norm = jnp.sqrt(total)
        norms[ll] = norm
        scale = jnp.minimum(1.0, 1.0 / (norm + 1e-06)) * factor
        for e in range(2):
            one = scale[e:e + 1, 0:1]

            @pl.loop(0, tokens // part_rows)
            def _(m):
                rows = pl.ds(pl.multiple_of(m * part_rows, part_rows), part_rows)
                value = b_buf[2 * ll + e, rows, :].astype(jnp.float32) * one
                b_buf[2 * ll + e, rows, :] = value.astype(jnp.bfloat16)

    def s_copy(block):
        hh, ll = block // L, block % L
        slot = (h - hh + H) % H - 1
        return pltpu.make_async_remote_copy(
            src_ref=c_buf.at[pl.ds(pl.multiple_of(block * RB, 16), RB)],
            dst_ref=recv.at[slot, pl.ds(pl.multiple_of(ll * RB, 16), RB)],
            send_sem=s_send.at[block], recv_sem=s_recv.at[slot, ll],
            device_id=(hh * L + l, s), device_id_type=MESH)

    chunk = 384
    for i, tile in enumerate(order):
        if i:
            spreads[i].finish()
            a_load(i).start()
        a_load(i).wait()

        @pl.loop(0, TM // chunk)
        def _(m):
            column = pl.multiple_of(m * chunk, 128)
            left = a_buf[i % 2, :, :, pl.ds(column, chunk)].reshape(examples * tokens, chunk)
            value = lax.dot_general(
                left, b_buf[...].reshape(examples * tokens, nb),
                (((0,), (0,)), ((), ())), preferred_element_type=jnp.float32)
            row = pl.multiple_of(tile * TM + m * chunk, 128)
            c_buf[pl.ds(row, chunk), :] = value.astype(jnp.bfloat16)

        for j in range(k):
            block = tile * k + j
            if L % k == 0:
                if i < tiles - L // k:
                    s_copy(block).start()
            else:
                @pl.when(block // L != h)
                def _():
                    s_copy(block).start()
        if i + 1 < tiles:
            spreads[i + 1].forward()

    def o_copy(ll):
        src = c_buf.at[pl.ds(pl.multiple_of((h * L + ll) * RB, 16), RB)]
        return pltpu.make_async_remote_copy(
            src_ref=src, dst_ref=out.at[:, pl.ds(pl.multiple_of(l * nb, 128), nb)],
            send_sem=o_send.at[ll], recv_sem=o_recv.at[l],
            device_id=(h * L + ll, s), device_id_type=MESH)

    own = pltpu.make_async_copy(
        c_buf.at[pl.ds(pl.multiple_of((h * L + l) * RB, 16), RB)],
        out.at[:, pl.ds(pl.multiple_of(l * nb, 128), nb)], own_sem)
    step = 96
    for ll in range(L):
        for slot in range(H - 1):
            landed(recv.at[slot, pl.ds(ll * RB, RB)], s_recv.at[slot, ll], d, s).wait_recv()

        @pl.loop(0, RB // step)
        def _(m):
            here = pl.ds(pl.multiple_of((h * L + ll) * RB + m * step, 16), step)
            there = pl.ds(pl.multiple_of(ll * RB + m * step, 16), step)
            total = c_buf[here, :].astype(jnp.float32)
            for slot in range(H - 1):
                total = total + recv[slot, there, :].astype(jnp.float32)
            c_buf[here, :] = total.astype(jnp.bfloat16)

        @pl.when(l != ll)
        def _():
            o_copy(ll).start()

        @pl.when(l == ll)
        def _():
            own.start()
    for o in range(1, H):
        for ll in range(L):
            s_copy((h + o) % H * L + ll).wait_send()
    for j in range(1, L):
        ll = xor(l, j)
        land = out.at[:, pl.ds(pl.multiple_of(ll * nb, 128), nb)]
        landed(land, o_recv.at[ll], d, s).wait_recv()
        o_copy(ll).wait_send()
    own.wait()
    for copy in copies:
        copy.wait_send()


def product(dp, seq, L, factor, part, a_own, a_first, b_all):
    examples, tokens, nb = b_all.shape
    D = a_own.shape[2]
    H, RB = dp // L, D // dp
    TM = math.lcm(RB, 128)
    rest = D // TM - 1
    dma = pltpu.SemaphoreType.DMA
    vmem, anywhere = pl.BlockSpec(memory_space=pltpu.VMEM), pl.BlockSpec(memory_space=pl.ANY)
    return pl.pallas_call(
        functools.partial(product_kernel, H, L, seq, RB, TM, factor),
        out_shape=(
            jax.ShapeDtypeStruct((RB, nb * L), jnp.bfloat16),
            jax.ShapeDtypeStruct((L, 8, 128), jnp.float32),
            jax.ShapeDtypeStruct((rest, examples, tokens, TM), jnp.bfloat16),
        ),
        in_specs=[vmem, anywhere, anywhere, anywhere],
        out_specs=(anywhere, vmem, anywhere),
        scratch_shapes=[
            pltpu.VMEM((2, examples, tokens, TM), jnp.bfloat16),
            pltpu.VMEM((examples, tokens, nb), jnp.bfloat16),
            pltpu.VMEM((D, nb), jnp.bfloat16),
            pltpu.VMEM((H - 1, L * RB, nb), jnp.bfloat16),
            pltpu.VMEM((L * seq, 8, 128), jnp.float32),
            dma((L, seq)), dma((L, seq)),
            dma((rest, L)), dma((rest, L)), dma((rest, L)), dma((rest, L)), dma((rest, 2)),
            dma((2,)), dma, dma((dp,)), dma((H - 1, L)), dma((L,)), dma((L,)), dma,
        ],
        compiler_params=pltpu.CompilerParams(
            collective_id=1, has_side_effects=True, vmem_limit_bytes=60 * 2**20),
        cost_estimate=pl.CostEstimate(
            flops=2 * examples * tokens * D * nb,
            bytes_accessed=2 * (examples * tokens * (D + nb) + RB * nb * L), transcendentals=0),
        name="product_scatter",
    )(part, a_own, a_first, b_all)


def on_device(acts, grads):
    seq, dp = lax.axis_size("seq"), lax.axis_size("dp")
    examples, local_len, width = acts.shape
    hidden = grads.shape[2]
    L = split_of(dp, seq, hidden)
    a_own, a_first, b_own, b_all = gather(dp, seq, L, acts, grads)
    act_gram = jnp.einsum("nih,nfh->nif", a_own, a_own, preferred_element_type=jnp.float32)
    grad_gram = jnp.einsum("nih,nfh->nif", b_own, b_own, preferred_element_type=jnp.float32)
    part = jnp.sum(act_gram * grad_gram, axis=(1, 2))
    tile = jnp.pad(jnp.broadcast_to(part[:, None], (examples, 128)), ((0, 8 - examples), (0, 0)))
    factor = math.sqrt(width * hidden / (examples * dp))
    update, norms, _ = product(dp, seq, L, factor, tile, a_own, a_first, b_all)
    own = lax.dynamic_slice(norms, (lax.axis_index("dp") % L, 0, 0), (1, examples, 1))
    return update, own.reshape(examples)


def solution(mesh):
    return jax.shard_map(
        on_device,
        mesh=mesh,
        in_specs=(P("dp", "seq", None), P("dp", "seq", None)),
        out_specs=(P("dp", "seq"), P("dp")),
        check_vma=False,
    )
```

```python
import functools
import math

import jax
import jax.numpy as jnp
from jax import lax
from jax.experimental import pallas as pl
from jax.experimental.pallas import tpu as pltpu
from jax.sharding import PartitionSpec as P

MESH = pl.DeviceIdType.MESH
PARTS = 3


def flip(value, bit):
    return value + bit * (1 - 2 * ((value // bit) % 2))


def xor(value, mask):
    bit = 1
    while bit <= mask:
        if mask & bit:
            value = flip(value, bit)
        bit *= 2
    return value


def powers(count, first):
    found, bit = [], 1
    while bit < count:
        found.append(bit * first)
        bit *= 2
    return found


def split_of(dp, seq, hidden):
    lanes = dp // 2
    while (hidden // seq) % (lanes * 128):
        lanes //= 2
    return lanes


def gather_kernel(L, seq, acts, grads, a_all, b_all,
                  a_send, a_recv, f_send, f_recv, b_send, b_recv, own_sem):
    d, s = lax.axis_index("dp"), lax.axis_index("seq")
    h, l = d // L, d % L
    E, T, D = acts.shape
    nb = b_all.shape[2]
    W = D // PARTS
    bits = [("s", m) for m in powers(seq // 2, 2)] + [("l", m) for m in powers(L, 1)]
    n = len(bits)
    blocks = 1 << n

    def relative(mask, order, core=0):
        ll, ss = l, s
        for j in range(n):
            if mask >> j & 1:
                kind, m = order[j]
                if kind == "s":
                    ss = flip(ss, m)
                else:
                    ll = flip(ll, m)
        if core:
            ss = flip(ss, 1)
        return ll, ss

    barrier = pltpu.get_barrier_semaphore()
    for mask in range(blocks):
        for core in range(2):
            if mask or core:
                ll, ss = relative(mask, bits, core)
                pl.semaphore_signal(barrier, inc=1, device_id=(h * L + ll, ss), device_id_type=MESH)
    pl.semaphore_wait(barrier, 2 * blocks - 1)

    def a_at(ll, ss, r):
        return a_all.at[pl.ds(ll * E, E), pl.ds(ss * T, T), pl.ds(r * W, W)]

    def order_of(r):
        return bits[r % n:] + bits[:r % n]

    def a_copy(r, mask, k):
        order = order_of(r)
        src = acts.at[:, :, pl.ds(r * W, W)] if mask == 0 else a_at(*relative(mask, order), r)
        tl, ts = relative(1 << k, order)
        land = mask | 1 << k
        return pltpu.make_async_remote_copy(
            src_ref=src, dst_ref=a_at(*relative(mask, order), r),
            send_sem=a_send.at[r, land], recv_sem=a_recv.at[r, land],
            device_id=(h * L + tl, ts), device_id_type=MESH)

    def f_copy(r, mask):
        order = order_of(r)
        src = acts.at[:, :, pl.ds(r * W, W)] if mask == 0 else a_at(*relative(mask, order), r)
        tl, ts = relative(0, order, 1)
        return pltpu.make_async_remote_copy(
            src_ref=src, dst_ref=a_at(*relative(mask, order), r),
            send_sem=f_send.at[r, mask], recv_sem=f_recv.at[r, mask],
            device_id=(h * L + tl, ts), device_id_type=MESH)

    def landed(ref, sems, *index):
        return pltpu.make_async_remote_copy(
            src_ref=ref, dst_ref=ref, send_sem=sems.at[index], recv_sem=sems.at[index],
            device_id=(d, s), device_id_type=MESH)

    def b_copy(mask, core):
        tl, ts = relative(mask, bits, core)
        column = pl.multiple_of((ts * L + tl) * nb, 128)
        return pltpu.make_async_remote_copy(
            src_ref=grads.at[:, :, pl.ds(column, nb)],
            dst_ref=b_all.at[pl.ds(l * E, E), pl.ds(s * T, T), :],
            send_sem=b_send.at[mask, core], recv_sem=b_recv.at[mask, core],
            device_id=(h * L + tl, ts), device_id_type=MESH)

    started = []

    def go(copy):
        copy.start()
        started.append(copy)

    for k in range(n):
        for r in range(PARTS):
            go(a_copy(r, 0, k))
    own_a = pltpu.make_async_copy(
        acts, a_all.at[pl.ds(l * E, E), pl.ds(s * T, T), :], own_sem.at[0])
    own_a.start()
    column = pl.multiple_of((s * L + l) * nb, 128)
    own_b = pltpu.make_async_copy(
        grads.at[:, :, pl.ds(column, nb)],
        b_all.at[pl.ds(l * E, E), pl.ds(s * T, T), :], own_sem.at[1])
    own_b.start()
    for r in range(PARTS):
        go(f_copy(r, 0))
    to_send = sorted(
        ((m, c) for m in range(blocks) for c in range(2) if m or c),
        key=lambda mc: -bin(mc[0]).count("1"))
    half = len(to_send) // 2
    for mc in to_send[:half]:
        go(b_copy(*mc))
    arrivals = sorted(range(1, blocks), key=lambda m: (bin(m).count("1"), m))
    seen = 0
    for mask in arrivals:
        for r in range(PARTS):
            order = order_of(r)
            landed(a_at(*relative(mask, order), r), a_recv, r, mask).wait_recv()
            for k in range(mask.bit_length(), n):
                go(a_copy(r, mask, k))
            go(f_copy(r, mask))
        seen += 1
        if seen == n:
            for mc in to_send[half:]:
                go(b_copy(*mc))
    if seen < n:
        for mc in to_send[half:]:
            go(b_copy(*mc))
    for r in range(PARTS):
        order = order_of(r)
        for mask in range(blocks):
            landed(a_at(*relative(mask, order, 1), r), f_recv, r, mask).wait_recv()
    for mask, core in to_send:
        ll, ss = relative(mask, bits, core)
        landed(b_all.at[pl.ds(ll * E, E), pl.ds(ss * T, T), :], b_recv, mask, core).wait_recv()
    for copy in started:
        copy.wait_send()
    own_a.wait()
    own_b.wait()


def gather(L, seq, acts, grads):
    E, T, D = acts.shape
    nb = grads.shape[2] // (seq * L)
    blocks = L * seq // 2
    dma = pltpu.SemaphoreType.DMA
    return pl.pallas_call(
        functools.partial(gather_kernel, L, seq),
        out_shape=(
            jax.ShapeDtypeStruct((L * E, seq * T, D), acts.dtype),
            jax.ShapeDtypeStruct((L * E, seq * T, nb), grads.dtype),
        ),
        in_specs=[pl.BlockSpec(memory_space=pl.ANY)] * 2,
        out_specs=(pl.BlockSpec(memory_space=pl.ANY),) * 2,
        scratch_shapes=[
            dma((PARTS, blocks)), dma((PARTS, blocks)),
            dma((PARTS, blocks)), dma((PARTS, blocks)),
            dma((blocks, 2)), dma((blocks, 2)), dma((2,)),
        ],
        compiler_params=pltpu.CompilerParams(collective_id=0, has_side_effects=True),
        name="gather_tokens",
    )(acts, grads)


def landed_copy(ref, sem, d, s):
    return pltpu.make_async_remote_copy(
        src_ref=ref, dst_ref=ref, send_sem=sem, recv_sem=sem, device_id=(d, s), device_id_type=MESH)


CUTS = 3


def product_kernel(H, L, seq, RB, TM, factor, part, a_ref, b_ref, out, norms,
                   a_buf, b_buf, c_buf, recv, slots, n_send, n_recv,
                   a_sem, b_sem, s_send, s_recv, o_send, o_recv, own_sem):
    d, s = lax.axis_index("dp"), lax.axis_index("seq")
    h, l = d // L, d % L
    K, D = a_ref.shape
    nb = b_ref.shape[1]
    tiles, k, sub = D // TM, TM // RB, RB // CUTS
    whole_tiles = L % k == 0
    b_load = pltpu.make_async_copy(b_ref, b_buf, b_sem)
    b_load.start()
    if whole_tiles:
        per = L // k
        order = [((h + o) % H * per + xor(l // k, i), o != 0)
                 for o in list(range(1, H)) + [0] for i in reversed(range(per))]
    else:
        order = [(((h + 1) * L // k + i) % tiles, None) for i in range(tiles)]

    def a_load(i):
        column = pl.multiple_of(order[i][0] * TM, 128)
        return pltpu.make_async_copy(a_ref.at[:, pl.ds(column, TM)], a_buf.at[i % 2], a_sem.at[i % 2])

    a_load(0).start()
    group = [(j, q) for j in range(L) for q in range(seq) if j or q]
    barrier = pltpu.get_barrier_semaphore()
    for o in range(1, H):
        pl.semaphore_signal(barrier, inc=1, device_id=((h + o) % H * L + l, s), device_id_type=MESH)
    for j, q in group:
        pl.semaphore_signal(barrier, inc=1, device_id=(h * L + xor(l, j), xor(s, q)), device_id_type=MESH)
    pl.semaphore_wait(barrier, H - 1 + len(group))

    def n_copy(j, q):
        return pltpu.make_async_remote_copy(
            src_ref=part, dst_ref=slots.at[l * seq + s],
            send_sem=n_send.at[j, q], recv_sem=n_recv.at[j, q],
            device_id=(h * L + xor(l, j), xor(s, q)), device_id_type=MESH)

    for j, q in group:
        n_copy(j, q).start()
    slots[l * seq + s] = part[...]
    for j, q in group:
        landed_copy(slots.at[xor(l, j) * seq + xor(s, q)], n_recv.at[j, q], d, s).wait_recv()
    total = slots[0]
    for j in range(1, L * seq):
        total = total + slots[j]
    norm = jnp.sqrt(total)
    norms[...] = norm
    scale = jnp.minimum(1.0, 1.0 / (norm + 1e-06)) * factor
    b_load.wait()
    some = 64
    tokens = K // (2 * L)
    for e in range(2 * L):
        one = scale[e:e + 1, 0:1]

        @pl.loop(0, tokens // some)
        def _(m):
            rows = pl.ds(pl.multiple_of(e * tokens + m * some, some), some)
            b_buf[rows, :] = (b_buf[rows, :].astype(jnp.float32) * one).astype(jnp.bfloat16)

    def s_copy(piece):
        block = piece // CUTS
        hh, ll = block // L, block % L
        slot = (h - hh + H) % H - 1
        place = ll * CUTS + piece % CUTS
        return pltpu.make_async_remote_copy(
            src_ref=c_buf.at[pl.ds(pl.multiple_of(piece * sub, 16), sub)],
            dst_ref=recv.at[slot, pl.ds(pl.multiple_of(place * sub, 16), sub)],
            send_sem=s_send.at[piece], recv_sem=s_recv.at[slot, place],
            device_id=(hh * L + l, s), device_id_type=MESH)

    chunk = 384
    for i, (tile, away) in enumerate(order):
        if i + 1 < tiles:
            a_load(i + 1).start()
        a_load(i).wait()

        @pl.loop(0, TM // chunk)
        def _(m):
            column = pl.multiple_of(m * chunk, 128)
            value = lax.dot_general(
                a_buf[i % 2, :, pl.ds(column, chunk)], b_buf[...],
                (((0,), (0,)), ((), ())), preferred_element_type=jnp.float32)
            row = pl.multiple_of(tile * TM + m * chunk, 128)
            c_buf[pl.ds(row, chunk), :] = value.astype(jnp.bfloat16)
            for u in range(chunk // sub):
                piece = tile * (TM // sub) + m * (chunk // sub) + u
                if away is None:
                    @pl.when(piece // (CUTS * L) != h)
                    def _():
                        s_copy(piece).start()
                elif away:
                    s_copy(piece).start()

    def c_rows(place):
        return c_buf.at[pl.ds(pl.multiple_of((h * L * CUTS + place) * sub, 16), sub)]

    def o_copy(place):
        ll, u = place // CUTS, place % CUTS
        return pltpu.make_async_remote_copy(
            src_ref=c_rows(place),
            dst_ref=out.at[pl.ds(pl.multiple_of(u * sub, 16), sub), pl.ds(pl.multiple_of(l * nb, 128), nb)],
            send_sem=o_send.at[place], recv_sem=o_recv.at[l, u],
            device_id=(h * L + ll, s), device_id_type=MESH)

    def own(u):
        return pltpu.make_async_copy(
            c_rows(l * CUTS + u),
            out.at[pl.ds(u * sub, sub), pl.ds(pl.multiple_of(l * nb, 128), nb)], own_sem.at[u])

    if whole_tiles:
        places = [xor(l // k, i) * k * CUTS + j for i in reversed(range(per)) for j in range(k * CUTS)]
    else:
        places = list(range(L * CUTS))
    step = 96
    for at, place in enumerate(places):
        for slot in range(H - 1):
            land = recv.at[slot, pl.ds(pl.multiple_of(place * sub, 16), sub)]
            landed_copy(land, s_recv.at[slot, place], d, s).wait_recv()

        @pl.loop(0, sub // step)
        def _(m):
            here = pl.ds(pl.multiple_of((h * L * CUTS + place) * sub + m * step, 16), step)
            there = pl.ds(pl.multiple_of(place * sub + m * step, 16), step)
            value = c_buf[here, :].astype(jnp.float32)
            for slot in range(H - 1):
                value = value + recv[slot, there, :].astype(jnp.float32)
            c_buf[here, :] = value.astype(jnp.bfloat16)

        @pl.when(place // CUTS != l)
        def _():
            o_copy(place).start()

        @pl.when(place // CUTS == l)
        def _():
            own(at % CUTS).start()
    for j, q in group:
        n_copy(j, q).wait_send()
    for o in range(1, H):
        for place in range(L * CUTS):
            s_copy((h + o) % H * L * CUTS + place).wait_send()
    for j in range(1, L):
        ll = xor(l, j)
        for u in range(CUTS):
            land = out.at[pl.ds(u * sub, sub), pl.ds(pl.multiple_of(ll * nb, 128), nb)]
            landed_copy(land, o_recv.at[ll, u], d, s).wait_recv()
            o_copy(ll * CUTS + u).wait_send()
    for u in range(CUTS):
        own(u).wait()


def product(dp, seq, L, factor, part, a_all, b_all):
    K, D = a_all.shape
    nb = b_all.shape[1]
    H, RB = dp // L, D // dp
    TM = math.lcm(RB, 128)
    dma = pltpu.SemaphoreType.DMA
    vmem, anywhere = pl.BlockSpec(memory_space=pltpu.VMEM), pl.BlockSpec(memory_space=pl.ANY)
    return pl.pallas_call(
        functools.partial(product_kernel, H, L, seq, RB, TM, factor),
        out_shape=(
            jax.ShapeDtypeStruct((RB, nb * L), jnp.bfloat16),
            jax.ShapeDtypeStruct(part.shape, jnp.float32),
        ),
        in_specs=[vmem, anywhere, anywhere],
        out_specs=(anywhere, vmem),
        scratch_shapes=[
            pltpu.VMEM((2, K, TM), jnp.bfloat16),
            pltpu.VMEM((K, nb), jnp.bfloat16),
            pltpu.VMEM((D, nb), jnp.bfloat16),
            pltpu.VMEM((H - 1, L * RB, nb), jnp.bfloat16),
            pltpu.VMEM((L * seq,) + part.shape, jnp.float32),
            dma((L, seq)), dma((L, seq)),
            dma((2,)), dma, dma((dp * CUTS,)), dma((H - 1, L * CUTS)),
            dma((L * CUTS,)), dma((L, CUTS)), dma((CUTS,)),
        ],
        compiler_params=pltpu.CompilerParams(
            collective_id=1, has_side_effects=True, vmem_limit_bytes=60 * 2**20),
        cost_estimate=pl.CostEstimate(
            flops=2 * K * D * nb, bytes_accessed=2 * (K * D + K * nb + RB * nb * L), transcendentals=0),
        name="product_scatter",
    )(part, a_all, b_all)


def on_device(acts, grads):
    seq, dp = lax.axis_size("seq"), lax.axis_size("dp")
    examples, local_len, width = acts.shape
    hidden = grads.shape[2]
    L = split_of(dp, seq, hidden)
    a_all, b_all = gather(L, seq, acts, grads)
    act_gram = jnp.einsum("nih,nfh->nif", a_all, a_all, preferred_element_type=jnp.float32)
    grad_gram = jnp.einsum("nih,nfh->nif", b_all, b_all, preferred_element_type=jnp.float32)
    act_gram, grad_gram = lax.optimization_barrier((act_gram, grad_gram))
    part = jnp.sum(act_gram * grad_gram, axis=(1, 2))
    rows = -(-L * examples // 8) * 8
    tile = jnp.pad(jnp.broadcast_to(part[:, None], (L * examples, 128)), ((0, rows - L * examples), (0, 0)))
    factor = math.sqrt(width * hidden / (examples * dp))
    tokens = L * examples * seq * local_len
    update, norms = product(
        dp, seq, L, factor, tile, a_all.reshape(tokens, width), b_all.reshape(tokens, -1))
    own = lax.dynamic_slice(norms, (lax.axis_index("dp") % L * examples, 0), (examples, 1))
    return update, own.reshape(examples)


def solution(mesh):
    return jax.shard_map(
        on_device,
        mesh=mesh,
        in_specs=(P("dp", "seq", None), P("dp", "seq", None)),
        out_specs=(P("dp", "seq"), P("dp")),
        check_vma=False,
    )
```

```python
import functools
import math

import jax
import jax.numpy as jnp
from jax import lax
from jax.experimental import pallas as pl
from jax.experimental.pallas import tpu as pltpu
from jax.sharding import PartitionSpec as P

MESH = pl.DeviceIdType.MESH
PARTS = 3


def flip(value, bit):
    return value + bit * (1 - 2 * ((value // bit) % 2))


def xor(value, mask):
    bit = 1
    while bit <= mask:
        if mask & bit:
            value = flip(value, bit)
        bit *= 2
    return value


def powers(count, first):
    found, bit = [], 1
    while bit < count:
        found.append(bit * first)
        bit *= 2
    return found


def split_of(dp, seq, hidden):
    lanes = dp // 2
    while (hidden // seq) % (lanes * 128):
        lanes //= 2
    return lanes


def gather_kernel(L, seq, acts, grads, a_all, b_all,
                  a_send, a_recv, f_send, f_recv, b_send, b_recv, own_sem):
    d, s = lax.axis_index("dp"), lax.axis_index("seq")
    h, l = d // L, d % L
    E, T, D = acts.shape
    nb = b_all.shape[2]
    W = D // PARTS
    bits = [("s", m) for m in powers(seq // 2, 2)] + [("l", m) for m in powers(L, 1)]
    n = len(bits)
    blocks = 1 << n

    def relative(mask, order, core=0):
        ll, ss = l, s
        for j in range(n):
            if mask >> j & 1:
                kind, m = order[j]
                if kind == "s":
                    ss = flip(ss, m)
                else:
                    ll = flip(ll, m)
        if core:
            ss = flip(ss, 1)
        return ll, ss

    barrier = pltpu.get_barrier_semaphore()
    for mask in range(blocks):
        for core in range(2):
            if mask or core:
                ll, ss = relative(mask, bits, core)
                pl.semaphore_signal(barrier, inc=1, device_id=(h * L + ll, ss), device_id_type=MESH)
    pl.semaphore_wait(barrier, 2 * blocks - 1)

    def a_at(ll, ss, r):
        return a_all.at[pl.ds(ll * E, E), pl.ds(ss * T, T), pl.ds(r * W, W)]

    def order_of(r):
        return bits[r % n:] + bits[:r % n]

    def a_copy(r, mask, k):
        order = order_of(r)
        src = acts.at[:, :, pl.ds(r * W, W)] if mask == 0 else a_at(*relative(mask, order), r)
        tl, ts = relative(1 << k, order)
        land = mask | 1 << k
        return pltpu.make_async_remote_copy(
            src_ref=src, dst_ref=a_at(*relative(mask, order), r),
            send_sem=a_send.at[r, land], recv_sem=a_recv.at[r, land],
            device_id=(h * L + tl, ts), device_id_type=MESH)

    def f_copy(r, mask):
        order = order_of(r)
        src = acts.at[:, :, pl.ds(r * W, W)] if mask == 0 else a_at(*relative(mask, order), r)
        tl, ts = relative(0, order, 1)
        return pltpu.make_async_remote_copy(
            src_ref=src, dst_ref=a_at(*relative(mask, order), r),
            send_sem=f_send.at[r, mask], recv_sem=f_recv.at[r, mask],
            device_id=(h * L + tl, ts), device_id_type=MESH)

    def landed(ref, sems, *index):
        return pltpu.make_async_remote_copy(
            src_ref=ref, dst_ref=ref, send_sem=sems.at[index], recv_sem=sems.at[index],
            device_id=(d, s), device_id_type=MESH)

    def b_copy(mask, core):
        tl, ts = relative(mask, bits, core)
        column = pl.multiple_of((ts * L + tl) * nb, 128)
        return pltpu.make_async_remote_copy(
            src_ref=grads.at[:, :, pl.ds(column, nb)],
            dst_ref=b_all.at[pl.ds(l * E, E), pl.ds(s * T, T), :],
            send_sem=b_send.at[mask, core], recv_sem=b_recv.at[mask, core],
            device_id=(h * L + tl, ts), device_id_type=MESH)

    started = []

    def go(copy):
        copy.start()
        started.append(copy)

    for k in range(n):
        for r in range(PARTS):
            go(a_copy(r, 0, k))
    own_a = pltpu.make_async_copy(
        acts, a_all.at[pl.ds(l * E, E), pl.ds(s * T, T), :], own_sem.at[0])
    own_a.start()
    column = pl.multiple_of((s * L + l) * nb, 128)
    own_b = pltpu.make_async_copy(
        grads.at[:, :, pl.ds(column, nb)],
        b_all.at[pl.ds(l * E, E), pl.ds(s * T, T), :], own_sem.at[1])
    own_b.start()
    for r in range(PARTS):
        go(f_copy(r, 0))
    to_send = sorted(
        ((m, c) for m in range(blocks) for c in range(2) if m or c),
        key=lambda mc: -bin(mc[0]).count("1"))
    half = len(to_send) // 2
    for mc in to_send[:half]:
        go(b_copy(*mc))
    arrivals = sorted(range(1, blocks), key=lambda m: (bin(m).count("1"), m))
    seen = 0
    for mask in arrivals:
        for r in range(PARTS):
            order = order_of(r)
            landed(a_at(*relative(mask, order), r), a_recv, r, mask).wait_recv()
            for k in range(mask.bit_length(), n):
                go(a_copy(r, mask, k))
            go(f_copy(r, mask))
        seen += 1
        if seen == n:
            for mc in to_send[half:]:
                go(b_copy(*mc))
    if seen < n:
        for mc in to_send[half:]:
            go(b_copy(*mc))
    for r in range(PARTS):
        order = order_of(r)
        for mask in range(blocks):
            landed(a_at(*relative(mask, order, 1), r), f_recv, r, mask).wait_recv()
    for mask, core in to_send:
        ll, ss = relative(mask, bits, core)
        landed(b_all.at[pl.ds(ll * E, E), pl.ds(ss * T, T), :], b_recv, mask, core).wait_recv()
    for copy in started:
        copy.wait_send()
    own_a.wait()
    own_b.wait()


def gather(L, seq, acts, grads):
    E, T, D = acts.shape
    nb = grads.shape[2] // (seq * L)
    blocks = L * seq // 2
    dma = pltpu.SemaphoreType.DMA
    return pl.pallas_call(
        functools.partial(gather_kernel, L, seq),
        out_shape=(
            jax.ShapeDtypeStruct((L * E, seq * T, D), acts.dtype),
            jax.ShapeDtypeStruct((L * E, seq * T, nb), grads.dtype),
        ),
        in_specs=[pl.BlockSpec(memory_space=pl.ANY)] * 2,
        out_specs=(pl.BlockSpec(memory_space=pl.ANY),) * 2,
        scratch_shapes=[
            dma((PARTS, blocks)), dma((PARTS, blocks)),
            dma((PARTS, blocks)), dma((PARTS, blocks)),
            dma((blocks, 2)), dma((blocks, 2)), dma((2,)),
        ],
        compiler_params=pltpu.CompilerParams(collective_id=0, has_side_effects=True),
        name="gather_tokens",
    )(acts, grads)


def landed_copy(ref, sem, d, s):
    return pltpu.make_async_remote_copy(
        src_ref=ref, dst_ref=ref, send_sem=sem, recv_sem=sem, device_id=(d, s), device_id_type=MESH)


CUTS = 3


def product_kernel(H, L, seq, RB, TM, factor, part, a_ref, b_ref, out, norms,
                   a_buf, b_buf, c_buf, recv, slots, n_send, n_recv,
                   a_sem, b_sem, s_send, s_recv, o_send, o_recv, own_sem):
    d, s = lax.axis_index("dp"), lax.axis_index("seq")
    h, l = d // L, d % L
    K, D = a_ref.shape
    nb = b_ref.shape[1]
    tiles, k, sub = D // TM, TM // RB, RB // CUTS
    whole_tiles = L % k == 0
    b_load = pltpu.make_async_copy(b_ref, b_buf, b_sem)
    b_load.start()
    if whole_tiles:
        per = L // k
        order = [((h + o) % H * per + xor(l // k, i), o != 0)
                 for o in list(range(1, H)) + [0] for i in reversed(range(per))]
    else:
        order = [(((h + 1) * L // k + i) % tiles, None) for i in range(tiles)]

    def a_load(i):
        column = pl.multiple_of(order[i][0] * TM, 128)
        return pltpu.make_async_copy(a_ref.at[:, pl.ds(column, TM)], a_buf.at[i % 2], a_sem.at[i % 2])

    a_load(0).start()
    group = [(j, q) for j in range(L) for q in range(seq) if j or q]
    barrier = pltpu.get_barrier_semaphore()
    for o in range(1, H):
        pl.semaphore_signal(barrier, inc=1, device_id=((h + o) % H * L + l, s), device_id_type=MESH)
    for j, q in group:
        pl.semaphore_signal(barrier, inc=1, device_id=(h * L + xor(l, j), xor(s, q)), device_id_type=MESH)
    pl.semaphore_wait(barrier, H - 1 + len(group))

    def n_copy(j, q):
        return pltpu.make_async_remote_copy(
            src_ref=part, dst_ref=slots.at[l * seq + s],
            send_sem=n_send.at[j, q], recv_sem=n_recv.at[j, q],
            device_id=(h * L + xor(l, j), xor(s, q)), device_id_type=MESH)

    for j, q in group:
        n_copy(j, q).start()
    slots[l * seq + s] = part[...]
    for j, q in group:
        landed_copy(slots.at[xor(l, j) * seq + xor(s, q)], n_recv.at[j, q], d, s).wait_recv()
    total = slots[0]
    for j in range(1, L * seq):
        total = total + slots[j]
    norm = jnp.sqrt(total)
    norms[...] = norm
    scale = jnp.minimum(1.0, 1.0 / (norm + 1e-06)) * factor
    b_load.wait()
    some = 64
    tokens = K // (2 * L)
    for e in range(2 * L):
        one = scale[e:e + 1, 0:1]

        @pl.loop(0, tokens // some)
        def _(m):
            rows = pl.ds(pl.multiple_of(e * tokens + m * some, some), some)
            b_buf[rows, :] = (b_buf[rows, :].astype(jnp.float32) * one).astype(jnp.bfloat16)

    def s_copy(piece):
        block = piece // CUTS
        hh, ll = block // L, block % L
        slot = (h - hh + H) % H - 1
        place = ll * CUTS + piece % CUTS
        return pltpu.make_async_remote_copy(
            src_ref=c_buf.at[pl.ds(pl.multiple_of(piece * sub, 16), sub)],
            dst_ref=recv.at[slot, pl.ds(pl.multiple_of(place * sub, 16), sub)],
            send_sem=s_send.at[piece], recv_sem=s_recv.at[slot, place],
            device_id=(hh * L + l, s), device_id_type=MESH)

    chunk = 384
    for i, (tile, away) in enumerate(order):
        if i + 1 < tiles:
            a_load(i + 1).start()
        a_load(i).wait()

        @pl.loop(0, TM // chunk)
        def _(m):
            column = pl.multiple_of(m * chunk, 128)
            value = lax.dot_general(
                a_buf[i % 2, :, pl.ds(column, chunk)], b_buf[...],
                (((0,), (0,)), ((), ())), preferred_element_type=jnp.float32)
            row = pl.multiple_of(tile * TM + m * chunk, 128)
            c_buf[pl.ds(row, chunk), :] = value.astype(jnp.bfloat16)
            for u in range(chunk // sub):
                piece = tile * (TM // sub) + m * (chunk // sub) + u
                if away is None:
                    @pl.when(piece // (CUTS * L) != h)
                    def _():
                        s_copy(piece).start()
                elif away:
                    s_copy(piece).start()

    def c_rows(place):
        return c_buf.at[pl.ds(pl.multiple_of((h * L * CUTS + place) * sub, 16), sub)]

    def o_copy(place):
        ll, u = place // CUTS, place % CUTS
        return pltpu.make_async_remote_copy(
            src_ref=c_rows(place),
            dst_ref=out.at[pl.ds(pl.multiple_of(u * sub, 16), sub), pl.ds(pl.multiple_of(l * nb, 128), nb)],
            send_sem=o_send.at[place], recv_sem=o_recv.at[l, u],
            device_id=(h * L + ll, s), device_id_type=MESH)

    def own(u):
        return pltpu.make_async_copy(
            c_rows(l * CUTS + u),
            out.at[pl.ds(u * sub, sub), pl.ds(pl.multiple_of(l * nb, 128), nb)], own_sem.at[u])

    if whole_tiles:
        places = [xor(l // k, i) * k * CUTS + j for i in reversed(range(per)) for j in range(k * CUTS)]
    else:
        places = list(range(L * CUTS))
    step = 96
    for at, place in enumerate(places):
        for slot in range(H - 1):
            land = recv.at[slot, pl.ds(pl.multiple_of(place * sub, 16), sub)]
            landed_copy(land, s_recv.at[slot, place], d, s).wait_recv()

        @pl.loop(0, sub // step)
        def _(m):
            here = pl.ds(pl.multiple_of((h * L * CUTS + place) * sub + m * step, 16), step)
            there = pl.ds(pl.multiple_of(place * sub + m * step, 16), step)
            value = c_buf[here, :].astype(jnp.float32)
            for slot in range(H - 1):
                value = value + recv[slot, there, :].astype(jnp.float32)
            c_buf[here, :] = value.astype(jnp.bfloat16)

        @pl.when(place // CUTS != l)
        def _():
            o_copy(place).start()

        @pl.when(place // CUTS == l)
        def _():
            own(at % CUTS).start()
    for j, q in group:
        n_copy(j, q).wait_send()
    for o in range(1, H):
        for place in range(L * CUTS):
            s_copy((h + o) % H * L * CUTS + place).wait_send()
    for j in range(1, L):
        ll = xor(l, j)
        for u in range(CUTS):
            land = out.at[pl.ds(u * sub, sub), pl.ds(pl.multiple_of(ll * nb, 128), nb)]
            landed_copy(land, o_recv.at[ll, u], d, s).wait_recv()
            o_copy(ll * CUTS + u).wait_send()
    for u in range(CUTS):
        own(u).wait()


def product(dp, seq, L, factor, part, a_all, b_all):
    K, D = a_all.shape
    nb = b_all.shape[1]
    H, RB = dp // L, D // dp
    TM = math.lcm(RB, 128)
    dma = pltpu.SemaphoreType.DMA
    vmem, anywhere = pl.BlockSpec(memory_space=pltpu.VMEM), pl.BlockSpec(memory_space=pl.ANY)
    return pl.pallas_call(
        functools.partial(product_kernel, H, L, seq, RB, TM, factor),
        out_shape=(
            jax.ShapeDtypeStruct((RB, nb * L), jnp.bfloat16),
            jax.ShapeDtypeStruct(part.shape, jnp.float32),
        ),
        in_specs=[vmem, anywhere, anywhere],
        out_specs=(anywhere, vmem),
        scratch_shapes=[
            pltpu.VMEM((2, K, TM), jnp.bfloat16),
            pltpu.VMEM((K, nb), jnp.bfloat16),
            pltpu.VMEM((D, nb), jnp.bfloat16),
            pltpu.VMEM((H - 1, L * RB, nb), jnp.bfloat16),
            pltpu.VMEM((L * seq,) + part.shape, jnp.float32),
            dma((L, seq)), dma((L, seq)),
            dma((2,)), dma, dma((dp * CUTS,)), dma((H - 1, L * CUTS)),
            dma((L * CUTS,)), dma((L, CUTS)), dma((CUTS,)),
        ],
        compiler_params=pltpu.CompilerParams(
            collective_id=1, has_side_effects=True, vmem_limit_bytes=60 * 2**20),
        cost_estimate=pl.CostEstimate(
            flops=2 * K * D * nb, bytes_accessed=2 * (K * D + K * nb + RB * nb * L), transcendentals=0),
        name="product_scatter",
    )(part, a_all, b_all)


def gram_kernel(a_ref, b_ref, out):
    half = a_ref.shape[1] // 2

    def gram(ref, i, j):
        return lax.dot_general(
            ref[0, i * half:(i + 1) * half, :], ref[0, j * half:(j + 1) * half, :],
            (((1,), (1,)), ((), ())), preferred_element_type=jnp.float32)

    total = jnp.zeros((half, half), jnp.float32)
    for i, j, weight in ((0, 0, 1.0), (1, 0, 2.0), (1, 1, 1.0)):
        total = total + weight * (gram(a_ref, i, j) * gram(b_ref, i, j))
    whole = jnp.sum(jnp.sum(total, axis=0, keepdims=True), axis=1, keepdims=True)
    out[0] = jnp.broadcast_to(whole, out.shape[1:])


def squared_parts(a_all, b_all):
    count, tokens, width = a_all.shape
    nb = b_all.shape[2]
    return pl.pallas_call(
        gram_kernel,
        grid=(count,),
        out_shape=jax.ShapeDtypeStruct((count, 8, 128), jnp.float32),
        in_specs=[
            pl.BlockSpec((1, tokens, width), lambda i: (i, 0, 0)),
            pl.BlockSpec((1, tokens, nb), lambda i: (i, 0, 0)),
        ],
        out_specs=pl.BlockSpec((1, 8, 128), lambda i: (i, 0, 0)),
        compiler_params=pltpu.CompilerParams(vmem_limit_bytes=40 * 2**20),
        cost_estimate=pl.CostEstimate(
            flops=2 * count * tokens * tokens * (width + nb),
            bytes_accessed=2 * count * tokens * (width + nb), transcendentals=0),
        name="grams",
    )(a_all, b_all)


def on_device(acts, grads):
    seq, dp = lax.axis_size("seq"), lax.axis_size("dp")
    examples, local_len, width = acts.shape
    hidden = grads.shape[2]
    L = split_of(dp, seq, hidden)
    a_all, b_all = gather(L, seq, acts, grads)
    part = squared_parts(a_all, b_all)
    rows = -(-L * examples // 8) * 8
    tile = jnp.pad(part[:, 0, :], ((0, rows - L * examples), (0, 0)))
    factor = math.sqrt(width * hidden / (examples * dp))
    tokens = L * examples * seq * local_len
    update, norms = product(
        dp, seq, L, factor, tile, a_all.reshape(tokens, width), b_all.reshape(tokens, -1))
    own = lax.dynamic_slice(norms, (lax.axis_index("dp") % L * examples, 0), (examples, 1))
    return update, own.reshape(examples)


def solution(mesh):
    return jax.shard_map(
        on_device,
        mesh=mesh,
        in_specs=(P("dp", "seq", None), P("dp", "seq", None)),
        out_specs=(P("dp", "seq"), P("dp")),
        check_vma=False,
    )
```
